256 devices in a mesh: gx: 32 (over y, z_lo, x), gz: 8 (over z_hi, core).
Axes of the slice: x: 4, y: 4, z: 8 (z_hi: 4, z_lo: 2; z = z_hi * 2 + z_lo), core: 2. Of those that a mesh axis runs over, the one named last changes fastest.
Arguments:
- modes: bfloat16 [2, 384, 384, 3, 128], P(None, 'gx', 'gz'), may hold values from -6 to 6
- wall_grad: bfloat16 [2, 384, 384, 3, 128], P(None, 'gx', 'gz'), may hold values from -6 to 6
Outputs:
- convective: float32 [128, 128, 128], P('gx', 'gz')
The draws below stay inside these ranges and needn't reach their ends.
All inputs are finite; a program needn't handle non-finite values.
Results may differ from the reference program's by a relative error of at most 0.0038.
Values may be sent and summed in bfloat16 or wider, within the bound.
A program may use at most 64 MiB of HBM per device.

```python
import math
import jax
import jax.numpy as jnp
from jax import lax

M = 128
PLANES = 2
NX = 384
NZ = 384


def block_scale(key, dims, shards, least, high):
    gain, own = 1.0, jax.random.fold_in(key, 6)
    for position, parts in shards:
        steps = jnp.exp(jax.random.uniform(jax.random.fold_in(own, position), (parts,), jnp.float32, least / len(shards), high / len(shards)))
        gain = gain * jnp.repeat(steps, dims[position] // parts).reshape([-1 if axis == position else 1 for axis in range(len(dims))])
    return gain


def normal_values(rng, dims, scale, reach, split=(), held_as=jnp.bfloat16):
    values = scale * jax.random.normal(rng, dims, jnp.float32)
    if split:
        values = values * block_scale(rng, dims, split, -0.22, 0.18)
    return jnp.clip(values, -reach, reach).astype(held_as)


def setup_inputs(seed: int = 0) -> dict:
    seeds = jax.random.split(jax.random.key(seed), 3)
    return {
        "modes": normal_values(seeds[0], (PLANES, NX, NZ, 3, M), 1.0, 6.0, ((1, 32), (2, 8))),
        "wall_grad": normal_values(seeds[1], (PLANES, NX, NZ, 3, M), 1.0, 6.0, ((1, 32), (2, 8))),
    }


def derive(field, axis):
    coefs = (0.75, -0.15, 1.0 / 60.0)
    total = jnp.zeros_like(field)
    for shift_by, coef in zip((1, 2, 3), coefs):
        total = total + coef * (jnp.roll(field, -shift_by, axis) - jnp.roll(field, shift_by, axis))
    return total

def reference(modes, wall_grad):
    weight = 1.0 / math.sqrt(PLANES * NX * NZ)
    result = jnp.zeros((M, M, M), jnp.float32)
    block = 4
    for plane in range(PLANES):
        phi = modes[plane]
        field = phi.astype(jnp.float32)
        grad_x = derive(field, 0).astype(jnp.bfloat16).reshape(-1, 3, M)
        grad_z = derive(field, 1).astype(jnp.bfloat16).reshape(-1, 3, M)
        grad_y = wall_grad[plane].reshape(-1, 3, M)
        flat = phi.reshape(-1, 3, M)
        points = flat.shape[0]
        left = flat.reshape(points * 3, M)

        def one_block(index):
            start = (index * block).astype(jnp.int32)
            adv = jnp.zeros((points, 3, block, M), jnp.float32)
            for comp, grad in enumerate((grad_x, grad_y, grad_z)):
                part = lax.dynamic_slice_in_dim(grad, start, block, 2).astype(jnp.float32)
                adv = adv + part[:, :, :, None] * flat[:, comp, None, None, :].astype(jnp.float32)
            adv = adv.astype(jnp.bfloat16).reshape(points * 3, block * M)
            prod = lax.dot_general(left, adv, (((0,), (0,)), ((), ())), preferred_element_type=jnp.float32)
            return jnp.transpose(prod.reshape(M, block, M), (1, 0, 2))
        blocks = lax.map(one_block, jnp.arange(M // block, dtype=jnp.int32))
        result = result + blocks.reshape(M, M, M)
    return result * weight
```

```python
import functools
import math

import jax
import jax.numpy as jnp
from jax import lax
from jax.experimental import pallas as pl
from jax.experimental.pallas import tpu as pltpu
from jax.sharding import PartitionSpec as P

M = 128
BF = jnp.bfloat16
F32 = jnp.float32
MESH = pl.DeviceIdType.MESH
WEIGHT = 1.0 / math.sqrt(2 * 384 * 384)
POINTS = 1152
PASSES = 16


def kernel(phi, phi5, wall, edges, out,
           xlo, xhi, zlo, zhi, zpad, gnat, phil, gt, own, rchip, xsend, rxy, zsend, rz,
           hs_sem, hr_sem, cs_sem, cr_sem, xs_sem, xr_sem, zs_sem, zr_sem):
    gx = lax.axis_index("gx")
    gz = lax.axis_index("gz")
    yy = gx // 8
    zl = (gx // 4) % 2
    xx = gx % 4
    zh = gz // 2
    core = gz % 2
    partner = (gx, zh * 2 + 1 - core)

    def xy_peer(dx, dy):
        return (((yy + dy) % 4) * 8 + zl * 4 + (xx + dx) % 4, gz)

    def z_peer(dz, zr):
        return (yy * 8 + ((zl + zr) % 2) * 4 + xx, ((zh + dz) % 4) * 2 + core)

    x_next = ((gx + 1) % 32, gz)
    x_prev = ((gx + 31) % 32, gz)
    z_next = (gx, (gz + 1) % 8)
    z_prev = (gx, (gz + 7) % 8)

    barrier = pltpu.get_barrier_semaphore()
    peers = [partner, x_next, x_prev, z_next, z_prev]
    peers += [xy_peer(d % 4, d // 4) for d in range(1, 16)]
    peers += [z_peer(d % 4, d // 4) for d in range(1, 8)]
    for peer in peers:
        pl.semaphore_signal(barrier, inc=1, device_id=peer, device_id_type=MESH)
    pl.semaphore_wait(barrier, len(peers))

    def remote(src, dst, ss, rs, dev):
        return pltpu.make_async_remote_copy(
            src_ref=src, dst_ref=dst, send_sem=ss, recv_sem=rs, device_id=dev, device_id_type=MESH)

    halos = [
        remote(phi5.at[:, :, 9:12], xlo, hs_sem.at[0], hr_sem.at[0], x_next),
        remote(phi5.at[:, :, 0:3], xhi, hs_sem.at[1], hr_sem.at[1], x_prev),
        remote(edges.at[1], zlo, hs_sem.at[2], hr_sem.at[2], z_next),
        remote(edges.at[0], zhi, hs_sem.at[3], hr_sem.at[3], z_prev),
    ]
    for h in halos:
        h.start()

    zero = jnp.zeros((128, 128), F32)
    for c in range(3):
        for b in range(4):
            for h in range(2):
                rows = slice(b * 256 + h * 128, b * 256 + h * 128 + 128)
                phil[b, c, :, h * 128:h * 128 + 128] = phi[c, rows, :].astype(F32).T.astype(BF)
                gt[3 * b + 1, c, :, h * 128:h * 128 + 128] = wall[c, rows, :].astype(F32).T
        tail = phi[c, 1024:1152, :].astype(F32).T.astype(BF)
        phil[4, c, :, 0:128] = tail
        phil[4, c, :, 128:256] = tail
        gt[12, c, :, 128:256] = wall[c, 1024:1152, :].astype(F32).T
        gt[13, c, :, 128:256] = zero

    def fill(s, carry):
        c, p = s // 2, s % 2
        for x in range(12):
            zpad[s * 12 + x, 8:56, :] = phi5[c, p, x].astype(F32)
        return carry

    lax.fori_loop(0, 6, fill, 0)

    for h in halos:
        h.wait()
    for r in range(3):
        zpad[:, 5 + r, :] = zlo[r, 0:72, :].astype(F32)
        zpad[:, 56 + r, :] = zhi[r, 0:72, :].astype(F32)

    coefs = (0.75, -0.15, 1.0 / 60.0)

    def grads(s, carry):
        c, p = s // 2, s % 2

        def at(x):
            if x < 0:
                return xlo[c, p, x + 3].astype(F32)
            if x >= 12:
                return xhi[c, p, x - 12].astype(F32)
            return phi5[c, p, x].astype(F32)

        for x in range(12):
            total = jnp.zeros((48, M), F32)
            for d, coef in zip((1, 2, 3), coefs):
                total = total + coef * (at(x + d) - at(x - d))
            gnat[0, c, pl.ds(p * 576 + x * 48, 48), :] = total.astype(BF)
            total = jnp.zeros((48, M), F32)
            for d, coef in zip((1, 2, 3), coefs):
                total = total + coef * (
                    zpad[s * 12 + x, 8 + d:56 + d, :] - zpad[s * 12 + x, 8 - d:56 - d, :])
            gnat[1, c, pl.ds(p * 576 + x * 48, 48), :] = total.astype(BF)
        return carry

    lax.fori_loop(0, 6, grads, 0)

    for c in range(3):
        for b in range(4):
            for h in range(2):
                rows = slice(b * 256 + h * 128, b * 256 + h * 128 + 128)
                for n, a in ((0, 0), (1, 2)):
                    gt[3 * b + a, c, :, h * 128:h * 128 + 128] = gnat[n, c, rows, :].astype(F32).T
        gt[12, c, :, 0:128] = gnat[0, c, 1024:1152, :].astype(F32).T
        gt[13, c, :, 0:128] = gnat[1, c, 1024:1152, :].astype(F32).T

    def offsets(half, e):
        dy = e // 2
        return 2 * (e % 2) + (dy + 1 + half) % 2, dy

    def chip_copy(n):
        return remote(own.at[n, :, 1 - core], rchip.at[n], cs_sem.at[n], cr_sem.at[n], partner)

    def xy_copy(n, e):
        dx, dy = offsets(n % 2, e)
        return remote(xsend.at[n, e], rxy.at[n, e], xs_sem.at[n, e], xr_sem.at[n, e], xy_peer(dx, dy))

    def z_copy(q, dz):
        zr, kk = q // 4, q % 4
        return remote(zsend.at[q, (zh + dz) % 4], rz.at[kk, zr * 4 + dz],
                      zs_sem.at[q, dz], zr_sem.at[q, dz], z_peer(dz, zr))

    def send_xy(n):
        chip_copy(n).wait_recv()
        for e in range(8):
            xsend[n, e] = (own[n, e, core] + rchip[n, e]).astype(BF)
        for e in range(8):
            if e:
                xy_copy(n, e).start()
            else:
                @pl.when(n % 2 == 0)
                def _():
                    xy_copy(n, 0).start()

                @pl.when(n % 2 == 1)
                def _():
                    rxy[n, 0] = xsend[n, 0]

    def send_z(q):
        for half in range(2):
            for e in range(half, 8):
                xy_copy(2 * q + half, e).wait_recv()
        for s in range(4):
            total = jnp.zeros((16, M), F32)
            for half in range(2):
                for e in range(8):
                    total = total + rxy[2 * q + half, e, s * 16:s * 16 + 16, :].astype(F32)
            zsend[q, s] = total
        zr, kk = q // 4, q % 4
        for dz in range(1, 4):
            z_copy(q, dz).start()

        @pl.when(zr == 1)
        def _():
            z_copy(q, 0).start()

        @pl.when(zr == 0)
        def _():
            rz[kk, 0] = zsend[q, zh]

    def compute(n):
        q, half = n // 2, n % 2
        zr, kk = q // 4, q % 4
        ks = []
        for e in range(8):
            dx, dy = offsets(half, e)
            ks.append(((yy + dy) % 4) * 32 + ((zl + zr) % 2) * 16 + ((xx + dx) % 4) * 4 + kk)

        def scoped(*accs):
            pad = jnp.zeros((256, M), BF)
            for t in range(14):
                if t < 12:
                    a, b = t % 3, t // 3
                    block = phi[a, b * 256:b * 256 + 256, :]
                    left = b
                elif t == 12:
                    block = jnp.concatenate([phi[0, 1024:1152, :], phi[1, 1024:1152, :]], axis=0)
                    left = 4
                else:
                    block = jnp.concatenate([phi[2, 1024:1152, :], jnp.zeros((128, M), BF)], axis=0)
                    left = 4
                block = jnp.concatenate([block, pad], axis=1)
                for m in (0, 1):
                    pltpu.matmul_push_rhs(block, 0, m)
                ph = [phil[left, c] for c in range(3)]
                for kk4 in range(4):
                    for m in (0, 1):
                        e = m * 4 + kk4
                        rows = []
                        for c in range(3):
                            row = jnp.broadcast_to(gt[t, c, pl.ds(ks[e], 1), :], (8, 256)).astype(BF)
                            rows.append(jnp.concatenate([row] * 16, axis=0))
                        term = ph[0] * rows[0] + ph[1] * rows[1] + ph[2] * rows[2]
                        pltpu.matmul_acc_lhs(accs[e], term, load_staged_rhs=0 if kk4 == 0 else None)
            for e in range(8):
                res = pltpu.matmul_pop(accs[e])
                for s in range(8):
                    own[n, e, s % 2, (s // 2) * 16:(s // 2) * 16 + 16, :] = res[s * 16:s * 16 + 16, :M]

        pl.run_scoped(scoped, *[pltpu.ACC(e // 4)((128, 256), F32) for e in range(8)])
        chip_copy(n).start()

    def step(n, carry):
        compute(n)

        @pl.when(n >= 1)
        def _():
            send_xy(n - 1)

        @pl.when((n >= 3) & (n % 2 == 1))
        def _():
            send_z((n - 3) // 2)

        return carry

    lax.fori_loop(0, PASSES, step, 0)
    send_xy(PASSES - 1)
    send_z(PASSES // 2 - 1)

    for q in range(8):
        for dz in range(0 if q >= 4 else 1, 4):
            z_copy(q, dz).wait_recv()
    for kk in range(4):
        total = rz[kk, 0]
        for s in range(1, 8):
            total = total + rz[kk, s]
        out[kk] = total * WEIGHT

    def drain(n, carry):
        chip_copy(n).wait_send()
        for e in range(1, 8):
            xy_copy(n, e).wait_send()

        @pl.when(n % 2 == 0)
        def _():
            xy_copy(n, 0).wait_send()

        return carry

    lax.fori_loop(0, PASSES, drain, 0)
    for q in range(8):
        for dz in range(0 if q >= 4 else 1, 4):
            z_copy(q, dz).wait_send()


def per_device(modes, wall_grad):
    phi5 = jnp.transpose(modes, (3, 0, 1, 2, 4))
    wall = jnp.transpose(wall_grad, (3, 0, 1, 2, 4)).reshape(3, POINTS, M)
    rows = jnp.stack([modes[:, :, 0:3], modes[:, :, 45:48]])
    edges = jnp.transpose(rows, (0, 3, 4, 1, 2, 5)).reshape(2, 3, 72, M)
    edges = jnp.pad(edges, ((0, 0), (0, 0), (0, 8), (0, 0)))
    vm = pl.BlockSpec(memory_space=pltpu.VMEM)
    dma = pltpu.SemaphoreType.DMA
    return pl.pallas_call(
        kernel,
        out_shape=jax.ShapeDtypeStruct((4, 16, M), F32),
        in_specs=[vm] * 4,
        out_specs=vm,
        scratch_shapes=[
            pltpu.VMEM((3, 2, 3, 48, M), BF),
            pltpu.VMEM((3, 2, 3, 48, M), BF),
            pltpu.VMEM((3, 80, M), BF),
            pltpu.VMEM((3, 80, M), BF),
            pltpu.VMEM((72, 64, M), F32),
            pltpu.VMEM((2, 3, POINTS, M), BF),
            pltpu.VMEM((5, 3, M, 256), BF),
            pltpu.VMEM((14, 3, M, 256), F32),
            pltpu.VMEM((PASSES, 8, 2, 64, M), F32),
            pltpu.VMEM((PASSES, 8, 64, M), F32),
            pltpu.VMEM((PASSES, 8, 64, M), BF),
            pltpu.VMEM((PASSES, 8, 64, M), BF),
            pltpu.VMEM((8, 4, 16, M), F32),
            pltpu.VMEM((4, 8, 16, M), F32),
            dma((4,)), dma((4,)),
            dma((PASSES,)), dma((PASSES,)),
            dma((PASSES, 8)), dma((PASSES, 8)),
            dma((8, 4)), dma((8, 4)),
        ],
        compiler_params=pltpu.CompilerParams(
            collective_id=0, has_side_effects=True, vmem_limit_bytes=56 * 2**20),
        cost_estimate=pl.CostEstimate(
            flops=2 * 128 * 3456 * 16384, bytes_accessed=4 * 2**20, transcendentals=0),
    )(phi5.reshape(3, POINTS, M), phi5, wall, edges)


def solution(mesh):
    placed = (P(None, "gx", "gz", None, None), P(None, "gx", "gz", None, None))
    body = jax.shard_map(
        per_device, mesh=mesh, in_specs=placed, out_specs=P("gx", "gz", None), check_vma=False)

    def run(modes, wall_grad):
        with jax.sharding.use_abstract_mesh(mesh.abstract_mesh):
            return body(modes, wall_grad)

    return run
```

```python
import functools
import math

import jax
import jax.numpy as jnp
from jax import lax
from jax.experimental import pallas as pl
from jax.experimental.pallas import tpu as pltpu
from jax.sharding import PartitionSpec as P

M = 128
BF = jnp.bfloat16
F32 = jnp.float32
MESH = pl.DeviceIdType.MESH
WEIGHT = 1.0 / math.sqrt(2 * 384 * 384)
POINTS = 1152
PASSES = 16
EARLY = 5


def kernel(phi, phi5, wall, out,
           edges, xlo, xhi, zlo, zhi, zpad, gnat, phil, gt, own, rchip,
           sa1, sb1, ra1, rb1, sa2, sb2, ra2, rb2, zsend, rz,
           hs_sem, hr_sem, cs_sem, cr_sem, a1s, a1r, b1s, b1r, a2s, a2r, b2s, b2r, zs_sem, zr_sem):
    gx = lax.axis_index("gx")
    gz = lax.axis_index("gz")
    yy = gx // 8
    zl = (gx // 4) % 2
    xx = gx % 4
    zh = gz // 2
    core = gz % 2
    partner = (gx, zh * 2 + 1 - core)

    def x_peer(dx):
        return (yy * 8 + zl * 4 + (xx + dx) % 4, gz)

    def y_peer(dy):
        return (((yy + dy) % 4) * 8 + zl * 4 + xx, gz)

    def z_peer(dz, zr):
        return (yy * 8 + ((zl + zr) % 2) * 4 + xx, ((zh + dz) % 4) * 2 + core)

    x_next = ((gx + 1) % 32, gz)
    x_prev = ((gx + 31) % 32, gz)
    z_next = (gx, (gz + 1) % 8)
    z_prev = (gx, (gz + 7) % 8)

    barrier = pltpu.get_barrier_semaphore()
    peers = [partner, x_next, x_prev, z_next, z_prev]
    peers += [x_peer(d) for d in range(1, 4)] + [y_peer(d) for d in range(1, 4)]
    peers += [z_peer(d % 4, d // 4) for d in range(1, 8)]
    for peer in peers:
        pl.semaphore_signal(barrier, inc=1, device_id=peer, device_id_type=MESH)

    def remote(src, dst, ss, rs, dev):
        return pltpu.make_async_remote_copy(
            src_ref=src, dst_ref=dst, send_sem=ss, recv_sem=rs, device_id=dev, device_id_type=MESH)

    zero = jnp.zeros((M, M), F32)
    for c in range(3):
        for b in range(4):
            for h in range(2):
                rows = slice(b * 256 + h * 128, b * 256 + h * 128 + 128)
                phil[b, c, :, h * 128:h * 128 + 128] = phi[c, rows, :].astype(F32).T.astype(BF)
                gt[b, c, :, h * 128:h * 128 + 128] = wall[c, rows, :].astype(F32).T
        tail = phi[c, 1024:1152, :].astype(F32).T.astype(BF)
        phil[4, c, :, 0:128] = tail
        phil[4, c, :, 128:256] = tail
        gt[4, c, :, 0:128] = wall[c, 1024:1152, :].astype(F32).T
        gt[4, c, :, 128:256] = zero

    def fill(s, carry):
        c, p = s // 2, s % 2
        for x in range(12):
            zpad[s * 12 + x, 8:56, :] = phi5[c, p, x].astype(F32)
        return carry

    lax.fori_loop(0, 6, fill, 0)
    for r in range(3):
        edges[0, r, 0:72, :] = zpad[:, 8 + r, :].astype(BF)
        edges[1, r, 0:72, :] = zpad[:, 53 + r, :].astype(BF)
        for side in range(2):
            edges[side, r, 72:80, :] = jnp.zeros((8, M), BF)

    def modes_of(n):
        q, half = n // 2, n % 2
        zr, kk = q // 4, q % 4
        ks = []
        for e in range(8):
            dx, dy = e % 4, 2 * (e // 4) + 1 - half
            ks.append(((yy + dy) % 4) * 32 + ((zl + zr) % 2) * 16 + ((xx + dx) % 4) * 4 + kk)
        return ks

    def contract(n, tiles, first):
        ks = modes_of(n)

        def scoped(*accs):
            for t, left, parts in tiles:
                block = [phi[a, lo:lo + size, :] for a, lo, size in parts]
                size = sum(p[2] for p in parts)
                if size < 256:
                    block.append(jnp.zeros((256 - size, M), BF))
                block = jnp.concatenate(block, axis=0) if len(block) > 1 else block[0]
                block = jnp.concatenate([block, jnp.zeros((256, M), BF)], axis=1)
                for m in (0, 1):
                    pltpu.matmul_push_rhs(block, 0, m)
                ph = [phil[left, c] for c in range(3)]
                for j in range(4):
                    for m in (0, 1):
                        e = m * 4 + j
                        rows = []
                        for c in range(3):
                            row = jnp.broadcast_to(gt[t, c, pl.ds(ks[e], 1), :], (8, 256)).astype(BF)
                            rows.append(jnp.concatenate([row] * 16, axis=0))
                        term = ph[0] * rows[0] + ph[1] * rows[1] + ph[2] * rows[2]
                        pltpu.matmul_acc_lhs(accs[e], term, load_staged_rhs=0 if j == 0 else None)
            for e in range(8):
                res = pltpu.matmul_pop(accs[e])
                for s in range(8):
                    piece = res[s * 16:s * 16 + 16, :M]
                    spot = slice((s // 2) * 16, (s // 2) * 16 + 16)
                    if not first:
                        piece = piece + own[n, e, s % 2, spot, :]
                    own[n, e, s % 2, spot, :] = piece

        pl.run_scoped(scoped, *[pltpu.ACC(e // 4)((M, 256), F32) for e in range(8)])

    y_tiles = [(b, b, [(1, b * 256, 256)]) for b in range(4)] + [(4, 4, [(1, 1024, 128)])]
    xz_tiles = []
    for b in range(4):
        xz_tiles += [(5 + 2 * b, b, [(0, b * 256, 256)]), (6 + 2 * b, b, [(2, b * 256, 256)])]
    xz_tiles.append((13, 4, [(0, 1024, 128), (2, 1024, 128)]))

    def wall_pass(n, carry):
        contract(n, y_tiles, True)
        return carry

    lax.fori_loop(0, EARLY, wall_pass, 0)
    pl.semaphore_wait(barrier, len(peers))
    halos = [
        remote(phi5.at[:, :, 9:12], xlo, hs_sem.at[0], hr_sem.at[0], x_next),
        remote(phi5.at[:, :, 0:3], xhi, hs_sem.at[1], hr_sem.at[1], x_prev),
        remote(edges.at[1], zlo, hs_sem.at[2], hr_sem.at[2], z_next),
        remote(edges.at[0], zhi, hs_sem.at[3], hr_sem.at[3], z_prev),
    ]
    for h in halos:
        h.start()
    lax.fori_loop(EARLY, PASSES, wall_pass, 0)
    for h in halos:
        h.wait()

    for r in range(3):
        zpad[:, 5 + r, :] = zlo[r, 0:72, :].astype(F32)
        zpad[:, 56 + r, :] = zhi[r, 0:72, :].astype(F32)

    coefs = (0.75, -0.15, 1.0 / 60.0)

    def grads(s, carry):
        c, p = s // 2, s % 2

        def at(x):
            if x < 0:
                return xlo[c, p, x + 3].astype(F32)
            if x >= 12:
                return xhi[c, p, x - 12].astype(F32)
            return phi5[c, p, x].astype(F32)

        for x in range(12):
            total = jnp.zeros((48, M), F32)
            for d, coef in zip((1, 2, 3), coefs):
                total = total + coef * (at(x + d) - at(x - d))
            gnat[0, c, pl.ds(p * 576 + x * 48, 48), :] = total.astype(BF)
            total = jnp.zeros((48, M), F32)
            for d, coef in zip((1, 2, 3), coefs):
                total = total + coef * (
                    zpad[s * 12 + x, 8 + d:56 + d, :] - zpad[s * 12 + x, 8 - d:56 - d, :])
            gnat[1, c, pl.ds(p * 576 + x * 48, 48), :] = total.astype(BF)
        return carry

    lax.fori_loop(0, 6, grads, 0)

    for c in range(3):
        for b in range(4):
            for h in range(2):
                rows = slice(b * 256 + h * 128, b * 256 + h * 128 + 128)
                for a in range(2):
                    gt[5 + 2 * b + a, c, :, h * 128:h * 128 + 128] = gnat[a, c, rows, :].astype(F32).T
        gt[13, c, :, 0:128] = gnat[0, c, 1024:1152, :].astype(F32).T
        gt[13, c, :, 128:256] = gnat[1, c, 1024:1152, :].astype(F32).T

    def chip_copy(n):
        return remote(own.at[n, :, 1 - core], rchip.at[n], cs_sem.at[n], cr_sem.at[n], partner)

    def a1_copy(n, dx):
        return remote(sa1.at[n, dx], ra1.at[n, dx], a1s.at[n, dx], a1r.at[n, dx], x_peer(dx))

    def b1_copy(n, i):
        return remote(sb1.at[n, i], rb1.at[n, i], b1s.at[n, i], b1r.at[n, i], y_peer(2 * i + 1 - n % 2))

    def a2_copy(q, dy):
        return remote(sa2.at[q, dy], ra2.at[q, dy], a2s.at[q, dy], a2r.at[q, dy], y_peer(dy))

    def b2_copy(q, dx):
        return remote(sb2.at[q, dx], rb2.at[q, dx], b2s.at[q, dx], b2r.at[q, dx], x_peer(dx))

    def z_copy(q, dz):
        zr, kk = q // 4, q % 4
        return remote(zsend.at[q, (zh + dz) % 4], rz.at[kk, zr * 4 + dz],
                      zs_sem.at[q, dz], zr_sem.at[q, dz], z_peer(dz, zr))

    def first_stage(n):
        chip_copy(n).wait_recv()
        for e in range(8):
            total = own[n, e, core] + rchip[n, e]
            rchip[n, e] = total
            sa1[n, e % 4, e // 4] = total[0:32].astype(BF)
            sb1[n, e // 4, e % 4] = total[32:64].astype(BF)
        for dx in range(1, 4):
            a1_copy(n, dx).start()
        b1_copy(n, 1).start()

        @pl.when(n % 2 == 0)
        def _():
            b1_copy(n, 0).start()

    def second_stage(q):
        for half in range(2):
            n = 2 * q + half
            for dx in range(1, 4):
                a1_copy(n, dx).wait_recv()
            for i in range(half, 2):
                b1_copy(n, i).wait_recv()
        for dy in range(4):
            n, i = 2 * q + 1 - dy % 2, dy // 2
            total = rchip[n, i * 4, 0:32]
            for dx in range(1, 4):
                total = total + ra1[n, dx, i].astype(F32)
            sa2[q, dy] = total
        for dx in range(4):
            total = rchip[2 * q + 1, dx, 32:64]
            for dy in range(1, 4):
                total = total + rb1[2 * q + 1 - dy % 2, dy // 2, dx].astype(F32)
            sb2[q, dx] = total
        for d in range(1, 4):
            a2_copy(q, d).start()
            b2_copy(q, d).start()

    def third_stage(q):
        for d in range(1, 4):
            a2_copy(q, d).wait_recv()
            b2_copy(q, d).wait_recv()
        low, high = sa2[q, 0], sb2[q, 0]
        for d in range(1, 4):
            low = low + ra2[q, d]
            high = high + rb2[q, d]
        zsend[q, 0] = low[0:16]
        zsend[q, 1] = low[16:32]
        zsend[q, 2] = high[0:16]
        zsend[q, 3] = high[16:32]
        zr, kk = q // 4, q % 4
        for dz in range(1, 4):
            z_copy(q, dz).start()

        @pl.when(zr == 1)
        def _():
            z_copy(q, 0).start()

        @pl.when(zr == 0)
        def _():
            rz[kk, 0] = zsend[q, zh]

    def step(n, carry):
        contract(n, xz_tiles, False)
        chip_copy(n).start()

        @pl.when(n >= 1)
        def _():
            first_stage(n - 1)

        @pl.when((n >= 4) & (n % 2 == 0))
        def _():
            second_stage((n - 4) // 2)

        @pl.when((n >= 7) & (n % 2 == 1))
        def _():
            third_stage((n - 7) // 2)

        return carry

    lax.fori_loop(0, PASSES, step, 0)

    second_stage(6)
    first_stage(15)
    third_stage(5)
    third_stage(6)
    second_stage(7)
    third_stage(7)

    for q in range(8):
        for dz in range(0 if q >= 4 else 1, 4):
            z_copy(q, dz).wait_recv()
    for kk in range(4):
        total = rz[kk, 0]
        for s in range(1, 8):
            total = total + rz[kk, s]
        out[kk] = total * WEIGHT

    def drain(n, carry):
        chip_copy(n).wait_send()
        for dx in range(1, 4):
            a1_copy(n, dx).wait_send()
        b1_copy(n, 1).wait_send()

        @pl.when(n % 2 == 0)
        def _():
            b1_copy(n, 0).wait_send()

        return carry

    lax.fori_loop(0, PASSES, drain, 0)
    for q in range(8):
        for d in range(1, 4):
            a2_copy(q, d).wait_send()
            b2_copy(q, d).wait_send()
        for dz in range(0 if q >= 4 else 1, 4):
            z_copy(q, dz).wait_send()


def per_device(modes, wall_grad):
    phi5 = jnp.transpose(modes, (3, 0, 1, 2, 4))
    wall = jnp.transpose(wall_grad, (3, 0, 1, 2, 4)).reshape(3, POINTS, M)
    vm = pl.BlockSpec(memory_space=pltpu.VMEM)
    dma = pltpu.SemaphoreType.DMA
    return pl.pallas_call(
        kernel,
        out_shape=jax.ShapeDtypeStruct((4, 16, M), F32),
        in_specs=[vm] * 3,
        out_specs=vm,
        scratch_shapes=[
            pltpu.VMEM((2, 3, 80, M), BF),
            pltpu.VMEM((3, 2, 3, 48, M), BF),
            pltpu.VMEM((3, 2, 3, 48, M), BF),
            pltpu.VMEM((3, 80, M), BF),
            pltpu.VMEM((3, 80, M), BF),
            pltpu.VMEM((72, 64, M), F32),
            pltpu.VMEM((2, 3, POINTS, M), BF),
            pltpu.VMEM((5, 3, M, 256), BF),
            pltpu.VMEM((14, 3, M, 256), F32),
            pltpu.VMEM((PASSES, 8, 2, 64, M), F32),
            pltpu.VMEM((PASSES, 8, 64, M), F32),
            pltpu.VMEM((PASSES, 4, 2, 32, M), BF),
            pltpu.VMEM((PASSES, 2, 4, 32, M), BF),
            pltpu.VMEM((PASSES, 4, 2, 32, M), BF),
            pltpu.VMEM((PASSES, 2, 4, 32, M), BF),
            pltpu.VMEM((8, 4, 32, M), F32),
            pltpu.VMEM((8, 4, 32, M), F32),
            pltpu.VMEM((8, 4, 32, M), F32),
            pltpu.VMEM((8, 4, 32, M), F32),
            pltpu.VMEM((8, 4, 16, M), F32),
            pltpu.VMEM((4, 8, 16, M), F32),
            dma((4,)), dma((4,)),
            dma((PASSES,)), dma((PASSES,)),
            dma((PASSES, 4)), dma((PASSES, 4)),
            dma((PASSES, 2)), dma((PASSES, 2)),
            dma((8, 4)), dma((8, 4)),
            dma((8, 4)), dma((8, 4)),
            dma((8, 4)), dma((8, 4)),
        ],
        compiler_params=pltpu.CompilerParams(
            collective_id=0, has_side_effects=True, vmem_limit_bytes=56 * 2**20),
        cost_estimate=pl.CostEstimate(
            flops=2 * 128 * 3456 * 16384, bytes_accessed=4 * 2**20, transcendentals=0),
    )(phi5.reshape(3, POINTS, M), phi5, wall)


def solution(mesh):
    placed = (P(None, "gx", "gz", None, None), P(None, "gx", "gz", None, None))
    body = jax.shard_map(
        per_device, mesh=mesh, in_specs=placed, out_specs=P("gx", "gz", None), check_vma=False)

    def run(modes, wall_grad):
        with jax.sharding.use_abstract_mesh(mesh.abstract_mesh):
            return body(modes, wall_grad)

    return run
```

```python
import functools
import math

import jax
import jax.numpy as jnp
from jax import lax
from jax.experimental import pallas as pl
from jax.experimental.pallas import tpu as pltpu
from jax.sharding import PartitionSpec as P

M = 128
BF = jnp.bfloat16
F32 = jnp.float32
MESH = pl.DeviceIdType.MESH
WEIGHT = 1.0 / math.sqrt(2 * 384 * 384)
POINTS = 1152
PASSES = 16
EARLY = 5


def kernel(phi5, wall5, out,
           edges, xlo, xhi, zlo, zhi, zpad, gnat, phil, gt, own, rchip,
           sa1, sb1, ra1, rb1, sa2, sb2, ra2, rb2, zsend, rz,
           hs_sem, hr_sem, cs_sem, cr_sem, a1s, a1r, b1s, b1r, a2s, a2r, b2s, b2r, zs_sem, zr_sem):
    gx = lax.axis_index("gx")
    gz = lax.axis_index("gz")
    yy = gx // 8
    zl = (gx // 4) % 2
    xx = gx % 4
    zh = gz // 2
    core = gz % 2
    partner = (gx, zh * 2 + 1 - core)

    def x_peer(dx):
        return (yy * 8 + zl * 4 + (xx + dx) % 4, gz)

    def y_peer(dy):
        return (((yy + dy) % 4) * 8 + zl * 4 + xx, gz)

    def z_peer(dz, zr):
        return (yy * 8 + ((zl + zr) % 2) * 4 + xx, ((zh + dz) % 4) * 2 + core)

    x_next = ((gx + 1) % 32, gz)
    x_prev = ((gx + 31) % 32, gz)
    z_next = (gx, (gz + 1) % 8)
    z_prev = (gx, (gz + 7) % 8)

    barrier = pltpu.get_barrier_semaphore()
    peers = [partner, x_next, x_prev, z_next, z_prev]
    peers += [x_peer(d) for d in range(1, 4)] + [y_peer(d) for d in range(1, 4)]
    peers += [z_peer(d % 4, d // 4) for d in range(1, 8)]
    for peer in peers:
        pl.semaphore_signal(barrier, inc=1, device_id=peer, device_id_type=MESH)

    def cells(ref, c, lo, size):
        pieces, end = [], lo + size
        while lo < end:
            slab, start = lo // 48, lo % 48
            count = min(48 - start, end - lo)
            pieces.append(ref[slab // 12, slab % 12, c, start:start + count, :])
            lo += count
        return pieces

    def turned(ref, c, lo):
        return jnp.concatenate([p.astype(F32) for p in cells(ref, c, lo, M)], axis=0).T

    def remote(src, dst, ss, rs, dev):
        return pltpu.make_async_remote_copy(
            src_ref=src, dst_ref=dst, send_sem=ss, recv_sem=rs, device_id=dev, device_id_type=MESH)

    zero = jnp.zeros((M, M), F32)
    for c in range(3):
        for b in range(4):
            for h in range(2):
                spot = slice(h * 128, h * 128 + 128)
                phil[b, c, :, spot] = turned(phi5, c, b * 256 + h * 128).astype(BF)
                gt[b, c, :, spot] = turned(wall5, c, b * 256 + h * 128)
        tail = turned(phi5, c, 1024).astype(BF)
        phil[4, c, :, 0:128] = tail
        phil[4, c, :, 128:256] = tail
        gt[4, c, :, 0:128] = turned(wall5, c, 1024)
        gt[4, c, :, 128:256] = zero

    def fill(s, carry):
        c, p = s // 2, s % 2
        for x in range(12):
            zpad[s * 12 + x, 8:56, :] = phi5[p, x, c].astype(F32)
        return carry

    lax.fori_loop(0, 6, fill, 0)
    for r in range(3):
        edges[0, r, 0:72, :] = zpad[:, 8 + r, :].astype(BF)
        edges[1, r, 0:72, :] = zpad[:, 53 + r, :].astype(BF)
        for side in range(2):
            edges[side, r, 72:80, :] = jnp.zeros((8, M), BF)

    def modes_of(n):
        q, half = n // 2, n % 2
        zr, kk = q // 4, q % 4
        ks = []
        for e in range(8):
            dx, dy = e % 4, 2 * (e // 4) + 1 - half
            ks.append(((yy + dy) % 4) * 32 + ((zl + zr) % 2) * 16 + ((xx + dx) % 4) * 4 + kk)
        return ks

    def contract(n, tiles, first):
        ks = modes_of(n)

        def scoped(*accs):
            for t, left, parts in tiles:
                block = [p for a, lo, size in parts for p in cells(phi5, a, lo, size)]
                size = sum(p[2] for p in parts)
                if size < 256:
                    block.append(jnp.zeros((256 - size, M), BF))
                block = jnp.concatenate(block, axis=0)
                block = jnp.concatenate([block, jnp.zeros((256, M), BF)], axis=1)
                for m in (0, 1):
                    pltpu.matmul_push_rhs(block, 0, m)
                ph = [phil[left, c] for c in range(3)]
                for j in range(4):
                    for m in (0, 1):
                        e = m * 4 + j
                        rows = []
                        for c in range(3):
                            row = jnp.broadcast_to(gt[t, c, pl.ds(ks[e], 1), :], (8, 256)).astype(BF)
                            rows.append(jnp.concatenate([row] * 16, axis=0))
                        term = ph[0] * rows[0] + ph[1] * rows[1] + ph[2] * rows[2]
                        pltpu.matmul_acc_lhs(accs[e], term, load_staged_rhs=0 if j == 0 else None)
            for e in range(8):
                res = pltpu.matmul_pop(accs[e])
                for s in range(8):
                    piece = res[s * 16:s * 16 + 16, :M]
                    spot = slice((s // 2) * 16, (s // 2) * 16 + 16)
                    if not first:
                        piece = piece + own[n, e, s % 2, spot, :]
                    own[n, e, s % 2, spot, :] = piece

        pl.run_scoped(scoped, *[pltpu.ACC(e // 4)((M, 256), F32) for e in range(8)])

    y_tiles = [(b, b, [(1, b * 256, 256)]) for b in range(4)] + [(4, 4, [(1, 1024, 128)])]
    xz_tiles = []
    for b in range(4):
        xz_tiles += [(5 + 2 * b, b, [(0, b * 256, 256)]), (6 + 2 * b, b, [(2, b * 256, 256)])]
    xz_tiles.append((13, 4, [(0, 1024, 128), (2, 1024, 128)]))

    def wall_pass(n, carry):
        contract(n, y_tiles, True)
        return carry

    lax.fori_loop(0, EARLY, wall_pass, 0)
    pl.semaphore_wait(barrier, len(peers))
    halos = [
        remote(phi5.at[:, 9:12], xlo, hs_sem.at[0], hr_sem.at[0], x_next),
        remote(phi5.at[:, 0:3], xhi, hs_sem.at[1], hr_sem.at[1], x_prev),
        remote(edges.at[1], zlo, hs_sem.at[2], hr_sem.at[2], z_next),
        remote(edges.at[0], zhi, hs_sem.at[3], hr_sem.at[3], z_prev),
    ]
    for h in halos:
        h.start()
    lax.fori_loop(EARLY, PASSES, wall_pass, 0)
    for h in halos:
        h.wait()

    for r in range(3):
        zpad[:, 5 + r, :] = zlo[r, 0:72, :].astype(F32)
        zpad[:, 56 + r, :] = zhi[r, 0:72, :].astype(F32)

    coefs = (0.75, -0.15, 1.0 / 60.0)

    def grads(s, carry):
        c, p = s // 2, s % 2

        def at(x):
            if x < 0:
                return xlo[p, x + 3, c].astype(F32)
            if x >= 12:
                return xhi[p, x - 12, c].astype(F32)
            return phi5[p, x, c].astype(F32)

        for x in range(12):
            total = jnp.zeros((48, M), F32)
            for d, coef in zip((1, 2, 3), coefs):
                total = total + coef * (at(x + d) - at(x - d))
            gnat[0, c, pl.ds(p * 576 + x * 48, 48), :] = total.astype(BF)
            total = jnp.zeros((48, M), F32)
            for d, coef in zip((1, 2, 3), coefs):
                total = total + coef * (
                    zpad[s * 12 + x, 8 + d:56 + d, :] - zpad[s * 12 + x, 8 - d:56 - d, :])
            gnat[1, c, pl.ds(p * 576 + x * 48, 48), :] = total.astype(BF)
        return carry

    lax.fori_loop(0, 6, grads, 0)

    for c in range(3):
        for b in range(4):
            for h in range(2):
                rows = slice(b * 256 + h * 128, b * 256 + h * 128 + 128)
                for a in range(2):
                    gt[5 + 2 * b + a, c, :, h * 128:h * 128 + 128] = gnat[a, c, rows, :].astype(F32).T
        gt[13, c, :, 0:128] = gnat[0, c, 1024:1152, :].astype(F32).T
        gt[13, c, :, 128:256] = gnat[1, c, 1024:1152, :].astype(F32).T

    def chip_copy(n):
        return remote(own.at[n, :, 1 - core], rchip.at[n], cs_sem.at[n], cr_sem.at[n], partner)

    def a1_copy(n, dx):
        return remote(sa1.at[n, dx], ra1.at[n, dx], a1s.at[n, dx], a1r.at[n, dx], x_peer(dx))

    def b1_copy(n, i):
        return remote(sb1.at[n, i], rb1.at[n, i], b1s.at[n, i], b1r.at[n, i], y_peer(2 * i + 1 - n % 2))

    def a2_copy(q, dy):
        return remote(sa2.at[q, dy], ra2.at[q, dy], a2s.at[q, dy], a2r.at[q, dy], y_peer(dy))

    def b2_copy(q, dx):
        return remote(sb2.at[q, dx], rb2.at[q, dx], b2s.at[q, dx], b2r.at[q, dx], x_peer(dx))

    def z_copy(q, dz):
        zr, kk = q // 4, q % 4
        return remote(zsend.at[q, (zh + dz) % 4], rz.at[kk, zr * 4 + dz],
                      zs_sem.at[q, dz], zr_sem.at[q, dz], z_peer(dz, zr))

    def chip_sum(n):
        chip_copy(n).wait_recv()
        for e in range(8):
            total = own[n, e, core] + rchip[n, e]
            rchip[n, e] = total
            sa1[n, e % 4, e // 4] = total[0:32].astype(BF)
            sb1[n, e // 4, e % 4] = total[32:64].astype(BF)

    def first_stage(n):
        for dx in range(1, 4):
            a1_copy(n, dx).start()
        b1_copy(n, 1).start()

        @pl.when(n % 2 == 0)
        def _():
            b1_copy(n, 0).start()

    def second_stage(q):
        for half in range(2):
            n = 2 * q + half
            for dx in range(1, 4):
                a1_copy(n, dx).wait_recv()
            for i in range(half, 2):
                b1_copy(n, i).wait_recv()
        for dy in range(4):
            n, i = 2 * q + 1 - dy % 2, dy // 2
            total = rchip[n, i * 4, 0:32]
            for dx in range(1, 4):
                total = total + ra1[n, dx, i].astype(F32)
            sa2[q, dy] = total
        for dx in range(4):
            total = rchip[2 * q + 1, dx, 32:64]
            for dy in range(1, 4):
                total = total + rb1[2 * q + 1 - dy % 2, dy // 2, dx].astype(F32)
            sb2[q, dx] = total
        for d in range(1, 4):
            a2_copy(q, d).start()
            b2_copy(q, d).start()

    def third_stage(q):
        for d in range(1, 4):
            a2_copy(q, d).wait_recv()
            b2_copy(q, d).wait_recv()
        low, high = sa2[q, 0], sb2[q, 0]
        for d in range(1, 4):
            low = low + ra2[q, d]
            high = high + rb2[q, d]
        zsend[q, 0] = low[0:16]
        zsend[q, 1] = low[16:32]
        zsend[q, 2] = high[0:16]
        zsend[q, 3] = high[16:32]
        zr, kk = q // 4, q % 4
        for dz in range(1, 4):
            z_copy(q, dz).start()

        @pl.when(zr == 1)
        def _():
            z_copy(q, 0).start()

        @pl.when(zr == 0)
        def _():
            rz[kk, 0] = zsend[q, zh]

    def step(n, carry):
        chip_sum(n - 2)
        contract(n, xz_tiles, False)
        chip_copy(n).start()
        first_stage(n - 2)

        @pl.when((n >= 6) & (n % 2 == 0))
        def _():
            second_stage((n - 6) // 2)

        @pl.when((n >= 9) & (n % 2 == 1))
        def _():
            third_stage((n - 9) // 2)

        return carry

    def opening(n, carry):
        contract(n, xz_tiles, False)
        chip_copy(n).start()
        return carry

    lax.fori_loop(0, 2, opening, 0)
    lax.fori_loop(2, PASSES, step, 0)
    chip_sum(14)
    first_stage(14)

    second_stage(5)
    third_stage(4)
    chip_sum(15)
    first_stage(15)
    second_stage(6)
    third_stage(5)
    second_stage(7)
    third_stage(6)
    third_stage(7)

    for q in range(8):
        for dz in range(0 if q >= 4 else 1, 4):
            z_copy(q, dz).wait_recv()
    for kk in range(4):
        total = rz[kk, 0]
        for s in range(1, 8):
            total = total + rz[kk, s]
        out[kk] = total * WEIGHT

    def drain(n, carry):
        chip_copy(n).wait_send()
        for dx in range(1, 4):
            a1_copy(n, dx).wait_send()
        b1_copy(n, 1).wait_send()

        @pl.when(n % 2 == 0)
        def _():
            b1_copy(n, 0).wait_send()

        return carry

    lax.fori_loop(0, PASSES, drain, 0)
    for q in range(8):
        for d in range(1, 4):
            a2_copy(q, d).wait_send()
            b2_copy(q, d).wait_send()
        for dz in range(0 if q >= 4 else 1, 4):
            z_copy(q, dz).wait_send()


def per_device(modes, wall_grad):
    phi5 = jnp.transpose(modes, (0, 1, 3, 2, 4))
    wall5 = jnp.transpose(wall_grad, (0, 1, 3, 2, 4))
    vm = pl.BlockSpec(memory_space=pltpu.VMEM)
    dma = pltpu.SemaphoreType.DMA
    return pl.pallas_call(
        kernel,
        out_shape=jax.ShapeDtypeStruct((4, 16, M), F32),
        in_specs=[vm] * 2,
        out_specs=vm,
        scratch_shapes=[
            pltpu.VMEM((2, 3, 80, M), BF),
            pltpu.VMEM((2, 3, 3, 48, M), BF),
            pltpu.VMEM((2, 3, 3, 48, M), BF),
            pltpu.VMEM((3, 80, M), BF),
            pltpu.VMEM((3, 80, M), BF),
            pltpu.VMEM((72, 64, M), F32),
            pltpu.VMEM((2, 3, POINTS, M), BF),
            pltpu.VMEM((5, 3, M, 256), BF),
            pltpu.VMEM((14, 3, M, 256), F32),
            pltpu.VMEM((PASSES, 8, 2, 64, M), F32),
            pltpu.VMEM((PASSES, 8, 64, M), F32),
            pltpu.VMEM((PASSES, 4, 2, 32, M), BF),
            pltpu.VMEM((PASSES, 2, 4, 32, M), BF),
            pltpu.VMEM((PASSES, 4, 2, 32, M), BF),
            pltpu.VMEM((PASSES, 2, 4, 32, M), BF),
            pltpu.VMEM((8, 4, 32, M), F32),
            pltpu.VMEM((8, 4, 32, M), F32),
            pltpu.VMEM((8, 4, 32, M), F32),
            pltpu.VMEM((8, 4, 32, M), F32),
            pltpu.VMEM((8, 4, 16, M), F32),
            pltpu.VMEM((4, 8, 16, M), F32),
            dma((4,)), dma((4,)),
            dma((PASSES,)), dma((PASSES,)),
            dma((PASSES, 4)), dma((PASSES, 4)),
            dma((PASSES, 2)), dma((PASSES, 2)),
            dma((8, 4)), dma((8, 4)),
            dma((8, 4)), dma((8, 4)),
            dma((8, 4)), dma((8, 4)),
        ],
        compiler_params=pltpu.CompilerParams(
            collective_id=0, has_side_effects=True, vmem_limit_bytes=56 * 2**20),
        cost_estimate=pl.CostEstimate(
            flops=2 * 128 * 3456 * 16384, bytes_accessed=4 * 2**20, transcendentals=0),
    )(phi5, wall5)


def solution(mesh):
    placed = (P(None, "gx", "gz", None, None), P(None, "gx", "gz", None, None))
    body = jax.shard_map(
        per_device, mesh=mesh, in_specs=placed, out_specs=P("gx", "gz", None), check_vma=False)

    def run(modes, wall_grad):
        with jax.sharding.use_abstract_mesh(mesh.abstract_mesh):
            return body(modes, wall_grad)

    return run
```

```python
import functools
import math

import jax
import jax.numpy as jnp
from jax import lax
from jax.experimental import pallas as pl
from jax.experimental.pallas import tpu as pltpu
from jax.sharding import PartitionSpec as P

M = 128
BF = jnp.bfloat16
F32 = jnp.float32
MESH = pl.DeviceIdType.MESH
WEIGHT = 1.0 / math.sqrt(2 * 384 * 384)
POINTS = 1152
PASSES = 16
EARLY = 4


def kernel(phi5, wall5, out,
           edges, xlo, xhi, zlo, zhi, zpad, gnat, phil, gt, own, rchip,
           sa1, sb1, ra1, rb1, sa2, sb2, ra2, rb2, zsend, rz,
           hs_sem, hr_sem, cs_sem, cr_sem, a1s, a1r, b1s, b1r, a2s, a2r, b2s, b2r, zs_sem, zr_sem):
    gx = lax.axis_index("gx")
    gz = lax.axis_index("gz")
    yy = gx // 8
    zl = (gx // 4) % 2
    xx = gx % 4
    zh = gz // 2
    core = gz % 2
    partner = (gx, zh * 2 + 1 - core)

    def x_peer(dx):
        return (yy * 8 + zl * 4 + (xx + dx) % 4, gz)

    def y_peer(dy):
        return (((yy + dy) % 4) * 8 + zl * 4 + xx, gz)

    def z_peer(dz, zr):
        return (yy * 8 + ((zl + zr) % 2) * 4 + xx, ((zh + dz) % 4) * 2 + core)

    x_next = ((gx + 1) % 32, gz)
    x_prev = ((gx + 31) % 32, gz)
    z_next = (gx, (gz + 1) % 8)
    z_prev = (gx, (gz + 7) % 8)

    barrier = pltpu.get_barrier_semaphore()
    peers = [partner, x_next, x_prev, z_next, z_prev]
    peers += [x_peer(d) for d in range(1, 4)] + [y_peer(d) for d in range(1, 4)]
    peers += [z_peer(d % 4, d // 4) for d in range(1, 8)]
    for peer in peers:
        pl.semaphore_signal(barrier, inc=1, device_id=peer, device_id_type=MESH)

    def cells(ref, c, lo, size):
        pieces, end = [], lo + size
        while lo < end:
            slab, start = lo // 48, lo % 48
            count = min(48 - start, end - lo)
            pieces.append(ref[slab // 12, slab % 12, c, start:start + count, :])
            lo += count
        return pieces

    def turned(ref, c, lo):
        return jnp.concatenate([p.astype(F32) for p in cells(ref, c, lo, M)], axis=0).T

    def remote(src, dst, ss, rs, dev):
        return pltpu.make_async_remote_copy(
            src_ref=src, dst_ref=dst, send_sem=ss, recv_sem=rs, device_id=dev, device_id_type=MESH)

    zero = jnp.zeros((M, M), F32)
    for c in range(3):
        for b in range(4):
            for h in range(2):
                spot = slice(h * 128, h * 128 + 128)
                phil[b, c, :, spot] = turned(phi5, c, b * 256 + h * 128).astype(BF)
                gt[b, c, :, spot] = turned(wall5, c, b * 256 + h * 128)
        tail = turned(phi5, c, 1024).astype(BF)
        phil[4, c, :, 0:128] = tail
        phil[4, c, :, 128:256] = tail
        gt[4, c, :, 0:128] = turned(wall5, c, 1024)
        gt[4, c, :, 128:256] = zero

    def fill(s, carry):
        c, p = s // 2, s % 2
        for x in range(12):
            zpad[s * 12 + x, 8:56, :] = phi5[p, x, c].astype(F32)
        return carry

    lax.fori_loop(0, 6, fill, 0)
    for r in range(3):
        edges[0, r, 0:72, :] = zpad[:, 8 + r, :].astype(BF)
        edges[1, r, 0:72, :] = zpad[:, 53 + r, :].astype(BF)
        for side in range(2):
            edges[side, r, 72:80, :] = jnp.zeros((8, M), BF)

    def modes_of(n):
        q, half = n // 2, n % 2
        zr, kk = 1 - q // 4, q % 4
        ks = []
        for e in range(8):
            dx, dy = e % 4, 2 * (e // 4) + 1 - half
            ks.append(((yy + dy) % 4) * 32 + ((zl + zr) % 2) * 16 + ((xx + dx) % 4) * 4 + kk)
        return ks

    def contract(n, tiles, first):
        ks = modes_of(n)

        def scoped(*accs):
            for t, left, parts in tiles:
                block = [p for a, lo, size in parts for p in cells(phi5, a, lo, size)]
                size = sum(p[2] for p in parts)
                if size < 256:
                    block.append(jnp.zeros((256 - size, M), BF))
                block = jnp.concatenate(block, axis=0)
                block = jnp.concatenate([block, jnp.zeros((256, M), BF)], axis=1)
                for m in (0, 1):
                    pltpu.matmul_push_rhs(block, 0, m)
                ph = [phil[left, c] for c in range(3)]
                for j in range(4):
                    for m in (0, 1):
                        e = m * 4 + j
                        rows = []
                        for c in range(3):
                            row = jnp.broadcast_to(gt[t, c, pl.ds(ks[e], 1), :], (8, 256)).astype(BF)
                            rows.append(jnp.concatenate([row] * 16, axis=0))
                        term = ph[0] * rows[0] + ph[1] * rows[1] + ph[2] * rows[2]
                        pltpu.matmul_acc_lhs(accs[e], term, load_staged_rhs=0 if j == 0 else None)
            for e in range(8):
                res = pltpu.matmul_pop(accs[e])
                for s in range(8):
                    piece = res[s * 16:s * 16 + 16, :M]
                    spot = slice((s // 2) * 16, (s // 2) * 16 + 16)
                    if not first:
                        piece = piece + own[n, e, s % 2, spot, :]
                    own[n, e, s % 2, spot, :] = piece

        pl.run_scoped(scoped, *[pltpu.ACC(e // 4)((M, 256), F32) for e in range(8)])

    y_tiles = [(b, b, [(1, b * 256, 256)]) for b in range(4)] + [(4, 4, [(1, 1024, 128)])]
    xz_tiles = []
    for b in range(4):
        xz_tiles += [(5 + 2 * b, b, [(0, b * 256, 256)]), (6 + 2 * b, b, [(2, b * 256, 256)])]
    xz_tiles.append((13, 4, [(0, 1024, 128), (2, 1024, 128)]))

    def wall_pass(n, carry):
        contract(2 * n, y_tiles, True)
        contract(2 * n + 1, y_tiles, True)
        return carry

    lax.fori_loop(0, EARLY // 2, wall_pass, 0)
    pl.semaphore_wait(barrier, len(peers))
    halos = [
        remote(phi5.at[:, 9:12], xlo, hs_sem.at[0], hr_sem.at[0], x_next),
        remote(phi5.at[:, 0:3], xhi, hs_sem.at[1], hr_sem.at[1], x_prev),
        remote(edges.at[1], zlo, hs_sem.at[2], hr_sem.at[2], z_next),
        remote(edges.at[0], zhi, hs_sem.at[3], hr_sem.at[3], z_prev),
    ]
    for h in halos:
        h.start()
    lax.fori_loop(EARLY // 2, PASSES // 2, wall_pass, 0)
    for h in halos:
        h.wait()

    for r in range(3):
        zpad[:, 5 + r, :] = zlo[r, 0:72, :].astype(F32)
        zpad[:, 56 + r, :] = zhi[r, 0:72, :].astype(F32)

    coefs = (0.75, -0.15, 1.0 / 60.0)

    def grads(s, carry):
        c, p = s // 2, s % 2

        def at(x):
            if x < 0:
                return xlo[p, x + 3, c].astype(F32)
            if x >= 12:
                return xhi[p, x - 12, c].astype(F32)
            return phi5[p, x, c].astype(F32)

        for x in range(12):
            total = jnp.zeros((48, M), F32)
            for d, coef in zip((1, 2, 3), coefs):
                total = total + coef * (at(x + d) - at(x - d))
            gnat[0, c, pl.ds(p * 576 + x * 48, 48), :] = total.astype(BF)
            total = jnp.zeros((48, M), F32)
            for d, coef in zip((1, 2, 3), coefs):
                total = total + coef * (
                    zpad[s * 12 + x, 8 + d:56 + d, :] - zpad[s * 12 + x, 8 - d:56 - d, :])
            gnat[1, c, pl.ds(p * 576 + x * 48, 48), :] = total.astype(BF)
        return carry

    lax.fori_loop(0, 6, grads, 0)

    for c in range(3):
        for b in range(4):
            for h in range(2):
                rows = slice(b * 256 + h * 128, b * 256 + h * 128 + 128)
                for a in range(2):
                    gt[5 + 2 * b + a, c, :, h * 128:h * 128 + 128] = gnat[a, c, rows, :].astype(F32).T
        gt[13, c, :, 0:128] = gnat[0, c, 1024:1152, :].astype(F32).T
        gt[13, c, :, 128:256] = gnat[1, c, 1024:1152, :].astype(F32).T

    def chip_copy(n):
        return remote(own.at[n, :, 1 - core], rchip.at[n], cs_sem.at[n], cr_sem.at[n], partner)

    def a1_copy(n, dx):
        return remote(sa1.at[n, dx], ra1.at[n, dx], a1s.at[n, dx], a1r.at[n, dx], x_peer(dx))

    def b1_copy(n, i):
        return remote(sb1.at[n, i], rb1.at[n, i], b1s.at[n, i], b1r.at[n, i], y_peer(2 * i + 1 - n % 2))

    def a2_copy(q, dy):
        return remote(sa2.at[q, dy], ra2.at[q, dy], a2s.at[q, dy], a2r.at[q, dy], y_peer(dy))

    def b2_copy(q, dx):
        return remote(sb2.at[q, dx], rb2.at[q, dx], b2s.at[q, dx], b2r.at[q, dx], x_peer(dx))

    def z_copy(q, dz):
        zr, kk = 1 - q // 4, q % 4
        return remote(zsend.at[q, (zh + dz) % 4], rz.at[kk, zr * 4 + dz],
                      zs_sem.at[q, dz], zr_sem.at[q, dz], z_peer(dz, zr))

    def chip_sum(n):
        chip_copy(n).wait_recv()
        for e in range(8):
            total = own[n, e, core] + rchip[n, e]
            rchip[n, e] = total
            sa1[n, e % 4, e // 4] = total[0:32].astype(BF)
            sb1[n, e // 4, e % 4] = total[32:64].astype(BF)

    def first_stage(n):
        for dx in range(1, 4):
            a1_copy(n, dx).start()
        b1_copy(n, 1).start()

        @pl.when(n % 2 == 0)
        def _():
            b1_copy(n, 0).start()

    def second_stage(q):
        for half in range(2):
            n = 2 * q + half
            for dx in range(1, 4):
                a1_copy(n, dx).wait_recv()
            for i in range(half, 2):
                b1_copy(n, i).wait_recv()
        for dy in range(4):
            n, i = 2 * q + 1 - dy % 2, dy // 2
            total = rchip[n, i * 4, 0:32]
            for dx in range(1, 4):
                total = total + ra1[n, dx, i].astype(F32)
            sa2[q, dy] = total
        for dx in range(4):
            total = rchip[2 * q + 1, dx, 32:64]
            for dy in range(1, 4):
                total = total + rb1[2 * q + 1 - dy % 2, dy // 2, dx].astype(F32)
            sb2[q, dx] = total
        for d in range(1, 4):
            a2_copy(q, d).start()
            b2_copy(q, d).start()

    def third_stage(q):
        for d in range(1, 4):
            a2_copy(q, d).wait_recv()
            b2_copy(q, d).wait_recv()
        low, high = sa2[q, 0], sb2[q, 0]
        for d in range(1, 4):
            low = low + ra2[q, d]
            high = high + rb2[q, d]
        zsend[q, 0] = low[0:16]
        zsend[q, 1] = low[16:32]
        zsend[q, 2] = high[0:16]
        zsend[q, 3] = high[16:32]
        zr, kk = 1 - q // 4, q % 4
        for dz in range(1, 4):
            z_copy(q, dz).start()

        @pl.when(zr == 1)
        def _():
            z_copy(q, 0).start()

        @pl.when(zr == 0)
        def _():
            rz[kk, 0] = zsend[q, zh]

    def steps(m, carry):
        n = 2 * m
        chip_sum(n - 2)
        contract(n, xz_tiles, False)
        chip_copy(n).start()
        first_stage(n - 2)

        @pl.when(n >= 6)
        def _():
            second_stage(m - 3)

        chip_sum(n - 1)
        contract(n + 1, xz_tiles, False)
        chip_copy(n + 1).start()
        first_stage(n - 1)

        @pl.when(n >= 8)
        def _():
            third_stage(m - 4)

        return carry

    def opening(n, carry):
        contract(n, xz_tiles, False)
        chip_copy(n).start()
        return carry

    lax.fori_loop(0, 2, opening, 0)
    lax.fori_loop(1, PASSES // 2, steps, 0)
    chip_sum(14)
    first_stage(14)

    second_stage(5)
    third_stage(4)
    chip_sum(15)
    first_stage(15)
    second_stage(6)
    third_stage(5)
    second_stage(7)
    third_stage(6)
    third_stage(7)

    for q in range(8):
        for dz in range(0 if q < 4 else 1, 4):
            z_copy(q, dz).wait_recv()
    for kk in range(4):
        total = rz[kk, 0]
        for s in range(1, 8):
            total = total + rz[kk, s]
        out[kk] = total * WEIGHT

    def drain(n, carry):
        chip_copy(n).wait_send()
        for dx in range(1, 4):
            a1_copy(n, dx).wait_send()
        b1_copy(n, 1).wait_send()

        @pl.when(n % 2 == 0)
        def _():
            b1_copy(n, 0).wait_send()

        return carry

    lax.fori_loop(0, PASSES, drain, 0)
    for q in range(8):
        for d in range(1, 4):
            a2_copy(q, d).wait_send()
            b2_copy(q, d).wait_send()
        for dz in range(0 if q < 4 else 1, 4):
            z_copy(q, dz).wait_send()


def per_device(modes, wall_grad):
    phi5 = jnp.transpose(modes, (0, 1, 3, 2, 4))
    wall5 = jnp.transpose(wall_grad, (0, 1, 3, 2, 4))
    vm = pl.BlockSpec(memory_space=pltpu.VMEM)
    dma = pltpu.SemaphoreType.DMA
    return pl.pallas_call(
        kernel,
        out_shape=jax.ShapeDtypeStruct((4, 16, M), F32),
        in_specs=[vm] * 2,
        out_specs=vm,
        scratch_shapes=[
            pltpu.VMEM((2, 3, 80, M), BF),
            pltpu.VMEM((2, 3, 3, 48, M), BF),
            pltpu.VMEM((2, 3, 3, 48, M), BF),
            pltpu.VMEM((3, 80, M), BF),
            pltpu.VMEM((3, 80, M), BF),
            pltpu.VMEM((72, 64, M), F32),
            pltpu.VMEM((2, 3, POINTS, M), BF),
            pltpu.VMEM((5, 3, M, 256), BF),
            pltpu.VMEM((14, 3, M, 256), F32),
            pltpu.VMEM((PASSES, 8, 2, 64, M), F32),
            pltpu.VMEM((PASSES, 8, 64, M), F32),
            pltpu.VMEM((PASSES, 4, 2, 32, M), BF),
            pltpu.VMEM((PASSES, 2, 4, 32, M), BF),
            pltpu.VMEM((PASSES, 4, 2, 32, M), BF),
            pltpu.VMEM((PASSES, 2, 4, 32, M), BF),
            pltpu.VMEM((8, 4, 32, M), F32),
            pltpu.VMEM((8, 4, 32, M), F32),
            pltpu.VMEM((8, 4, 32, M), F32),
            pltpu.VMEM((8, 4, 32, M), F32),
            pltpu.VMEM((8, 4, 16, M), F32),
            pltpu.VMEM((4, 8, 16, M), F32),
            dma((4,)), dma((4,)),
            dma((PASSES,)), dma((PASSES,)),
            dma((PASSES, 4)), dma((PASSES, 4)),
            dma((PASSES, 2)), dma((PASSES, 2)),
            dma((8, 4)), dma((8, 4)),
            dma((8, 4)), dma((8, 4)),
            dma((8, 4)), dma((8, 4)),
        ],
        compiler_params=pltpu.CompilerParams(
            collective_id=0, has_side_effects=True, vmem_limit_bytes=56 * 2**20),
        cost_estimate=pl.CostEstimate(
            flops=2 * 128 * 3456 * 16384, bytes_accessed=4 * 2**20, transcendentals=0),
    )(phi5, wall5)


def solution(mesh):
    placed = (P(None, "gx", "gz", None, None), P(None, "gx", "gz", None, None))
    body = jax.shard_map(
        per_device, mesh=mesh, in_specs=placed, out_specs=P("gx", "gz", None), check_vma=False)

    def run(modes, wall_grad):
        with jax.sharding.use_abstract_mesh(mesh.abstract_mesh):
            return body(modes, wall_grad)

    return run
```

```python
import functools
import math

import jax
import jax.numpy as jnp
from jax import lax
from jax.experimental import pallas as pl
from jax.experimental.pallas import tpu as pltpu
from jax.sharding import PartitionSpec as P

M = 128
BF = jnp.bfloat16
F32 = jnp.float32
MESH = pl.DeviceIdType.MESH
WEIGHT = 1.0 / math.sqrt(2 * 384 * 384)
POINTS = 1152
PASSES = 16
EARLY = 6


def kernel(phi5, wall5, out,
           edges, xlo, xhi, zlo, zhi, zpad, gnat, phil, gt, own, rchip,
           sa1, sb1, ra1, rb1, sa2, sb2, ra2, rb2, zsend, rz,
           hs_sem, hr_sem, cs_sem, cr_sem, a1s, a1r, b1s, b1r, a2s, a2r, b2s, b2r, zs_sem, zr_sem):
    gx = lax.axis_index("gx")
    gz = lax.axis_index("gz")
    yy = gx // 8
    zl = (gx // 4) % 2
    xx = gx % 4
    zh = gz // 2
    core = gz % 2
    partner = (gx, zh * 2 + 1 - core)

    def x_peer(dx):
        return (yy * 8 + zl * 4 + (xx + dx) % 4, gz)

    def y_peer(dy):
        return (((yy + dy) % 4) * 8 + zl * 4 + xx, gz)

    def z_peer(dz, zr):
        return (yy * 8 + ((zl + zr) % 2) * 4 + xx, ((zh + dz) % 4) * 2 + core)

    x_next = ((gx + 1) % 32, gz)
    x_prev = ((gx + 31) % 32, gz)
    z_next = (gx, (gz + 1) % 8)
    z_prev = (gx, (gz + 7) % 8)

    barrier = pltpu.get_barrier_semaphore()
    peers = [partner, x_next, x_prev, z_next, z_prev]
    peers += [x_peer(d) for d in range(1, 4)] + [y_peer(d) for d in range(1, 4)]
    peers += [z_peer(d % 4, d // 4) for d in range(1, 8)]
    for peer in peers:
        pl.semaphore_signal(barrier, inc=1, device_id=peer, device_id_type=MESH)

    def cells(ref, c, lo, size):
        pieces, end = [], lo + size
        while lo < end:
            slab, start = lo // 48, lo % 48
            count = min(48 - start, end - lo)
            pieces.append(ref[slab // 12, slab % 12, c, start:start + count, :])
            lo += count
        return pieces

    def turned(ref, c, lo):
        return jnp.concatenate([p.astype(F32) for p in cells(ref, c, lo, M)], axis=0).T

    def remote(src, dst, ss, rs, dev):
        return pltpu.make_async_remote_copy(
            src_ref=src, dst_ref=dst, send_sem=ss, recv_sem=rs, device_id=dev, device_id_type=MESH)

    zero = jnp.zeros((M, M), F32)
    for c in range(3):
        for b in range(4):
            for h in range(2):
                spot = slice(h * 128, h * 128 + 128)
                phil[b, c, :, spot] = turned(phi5, c, b * 256 + h * 128).astype(BF)
                gt[b, c, :, spot] = turned(wall5, c, b * 256 + h * 128)
        tail = turned(phi5, c, 1024).astype(BF)
        phil[4, c, :, 0:128] = tail
        phil[4, c, :, 128:256] = tail
        gt[4, c, :, 0:128] = turned(wall5, c, 1024)
        gt[4, c, :, 128:256] = zero

    def fill(s, carry):
        c, p = s // 2, s % 2
        for x in range(12):
            zpad[s * 12 + x, 8:56, :] = phi5[p, x, c].astype(F32)
        return carry

    lax.fori_loop(0, 6, fill, 0)
    for r in range(3):
        edges[0, r, 0:72, :] = zpad[:, 8 + r, :].astype(BF)
        edges[1, r, 0:72, :] = zpad[:, 53 + r, :].astype(BF)
        for side in range(2):
            edges[side, r, 72:80, :] = jnp.zeros((8, M), BF)

    def modes_of(n):
        q, half = n // 2, n % 2
        zr, kk = 1 - q // 4, q % 4
        ks = []
        for e in range(8):
            dx, dy = e % 4, 2 * (e // 4) + 1 - half
            ks.append(((yy + dy) % 4) * 32 + ((zl + zr) % 2) * 16 + ((xx + dx) % 4) * 4 + kk)
        return ks

    def contract(n, tiles, first):
        ks = modes_of(n)

        def scoped(*accs):
            for t, left, parts in tiles:
                block = [p for a, lo, size in parts for p in cells(phi5, a, lo, size)]
                size = sum(p[2] for p in parts)
                if size < 256:
                    block.append(jnp.zeros((256 - size, M), BF))
                block = jnp.concatenate(block, axis=0)
                block = jnp.concatenate([block, jnp.zeros((256, M), BF)], axis=1)
                for m in (0, 1):
                    pltpu.matmul_push_rhs(block, 0, m)
                ph = [phil[left, c] for c in range(3)]
                for j in range(4):
                    for m in (0, 1):
                        e = m * 4 + j
                        rows = []
                        for c in range(3):
                            row = jnp.broadcast_to(gt[t, c, pl.ds(ks[e], 1), :], (8, 256)).astype(BF)
                            rows.append(jnp.concatenate([row] * 16, axis=0))
                        term = ph[0] * rows[0] + ph[1] * rows[1] + ph[2] * rows[2]
                        pltpu.matmul_acc_lhs(accs[e], term, load_staged_rhs=0 if j == 0 else None)
            for e in range(8):
                res = pltpu.matmul_pop(accs[e])
                for s in range(8):
                    piece = res[s * 16:s * 16 + 16, :M]
                    spot = slice((s // 2) * 16, (s // 2) * 16 + 16)
                    if not first:
                        piece = piece + own[n, e, s % 2, spot, :]
                    own[n, e, s % 2, spot, :] = piece

        pl.run_scoped(scoped, *[pltpu.ACC(e // 4)((M, 256), F32) for e in range(8)])

    y_tiles = [(b, b, [(1, b * 256, 256)]) for b in range(4)] + [(4, 4, [(1, 1024, 128)])]
    xz_tiles = []
    for b in range(4):
        xz_tiles += [(5 + 2 * b, b, [(0, b * 256, 256)]), (6 + 2 * b, b, [(2, b * 256, 256)])]
    xz_tiles.append((13, 4, [(0, 1024, 128), (2, 1024, 128)]))

    def wall_pass(n, carry):
        contract(2 * n, y_tiles, True)
        contract(2 * n + 1, y_tiles, True)
        return carry

    lax.fori_loop(0, EARLY // 2, wall_pass, 0)
    pl.semaphore_wait(barrier, len(peers))
    halos = [
        remote(phi5.at[:, 9:12], xlo, hs_sem.at[0], hr_sem.at[0], x_next),
        remote(phi5.at[:, 0:3], xhi, hs_sem.at[1], hr_sem.at[1], x_prev),
        remote(edges.at[1], zlo, hs_sem.at[2], hr_sem.at[2], z_next),
        remote(edges.at[0], zhi, hs_sem.at[3], hr_sem.at[3], z_prev),
    ]
    for h in halos:
        h.start()
    lax.fori_loop(EARLY // 2, PASSES // 2, wall_pass, 0)
    for h in halos:
        h.wait()

    for r in range(3):
        zpad[:, 5 + r, :] = zlo[r, 0:72, :].astype(F32)
        zpad[:, 56 + r, :] = zhi[r, 0:72, :].astype(F32)

    coefs = (0.75, -0.15, 1.0 / 60.0)

    def grads(s, carry):
        c, p = s // 2, s % 2

        def at(x):
            if x < 0:
                return xlo[p, x + 3, c].astype(F32)
            if x >= 12:
                return xhi[p, x - 12, c].astype(F32)
            return phi5[p, x, c].astype(F32)

        for x in range(12):
            total = jnp.zeros((48, M), F32)
            for d, coef in zip((1, 2, 3), coefs):
                total = total + coef * (at(x + d) - at(x - d))
            gnat[0, c, pl.ds(p * 576 + x * 48, 48), :] = total.astype(BF)
            total = jnp.zeros((48, M), F32)
            for d, coef in zip((1, 2, 3), coefs):
                total = total + coef * (
                    zpad[s * 12 + x, 8 + d:56 + d, :] - zpad[s * 12 + x, 8 - d:56 - d, :])
            gnat[1, c, pl.ds(p * 576 + x * 48, 48), :] = total.astype(BF)
        return carry

    lax.fori_loop(0, 6, grads, 0)

    for c in range(3):
        for b in range(4):
            for h in range(2):
                rows = slice(b * 256 + h * 128, b * 256 + h * 128 + 128)
                for a in range(2):
                    gt[5 + 2 * b + a, c, :, h * 128:h * 128 + 128] = gnat[a, c, rows, :].astype(F32).T
        gt[13, c, :, 0:128] = gnat[0, c, 1024:1152, :].astype(F32).T
        gt[13, c, :, 128:256] = gnat[1, c, 1024:1152, :].astype(F32).T

    def chip_copy(n):
        return remote(own.at[n, :, 1 - core], rchip.at[n], cs_sem.at[n], cr_sem.at[n], partner)

    def a1_copy(n, dx):
        return remote(sa1.at[n, dx], ra1.at[n, dx], a1s.at[n, dx], a1r.at[n, dx], x_peer(dx))

    def b1_copy(n, i):
        return remote(sb1.at[n, i], rb1.at[n, i], b1s.at[n, i], b1r.at[n, i], y_peer(2 * i + 1 - n % 2))

    def a2_copy(q, dy):
        return remote(sa2.at[q, dy], ra2.at[q, dy], a2s.at[q, dy], a2r.at[q, dy], y_peer(dy))

    def b2_copy(q, dx):
        return remote(sb2.at[q, dx], rb2.at[q, dx], b2s.at[q, dx], b2r.at[q, dx], x_peer(dx))

    def z_copy(q, dz):
        zr, kk = 1 - q // 4, q % 4
        return remote(zsend.at[q, (zh + dz) % 4], rz.at[kk, zr * 4 + dz],
                      zs_sem.at[q, dz], zr_sem.at[q, dz], z_peer(dz, zr))

    def chip_sum(n):
        chip_copy(n).wait_recv()
        for e in range(8):
            total = own[n, e, core] + rchip[n, e]
            rchip[n, e] = total
            sa1[n, e % 4, e // 4] = total[0:32].astype(BF)
            sb1[n, e // 4, e % 4] = total[32:64].astype(BF)

    def first_stage(n):
        for dx in range(1, 4):
            a1_copy(n, dx).start()
        b1_copy(n, 1).start()

        @pl.when(n % 2 == 0)
        def _():
            b1_copy(n, 0).start()

    def second_stage(q):
        for half in range(2):
            n = 2 * q + half
            for dx in range(1, 4):
                a1_copy(n, dx).wait_recv()
            for i in range(half, 2):
                b1_copy(n, i).wait_recv()
        for dy in range(4):
            n, i = 2 * q + 1 - dy % 2, dy // 2
            total = rchip[n, i * 4, 0:32]
            for dx in range(1, 4):
                total = total + ra1[n, dx, i].astype(F32)
            sa2[q, dy] = total
        for dx in range(4):
            total = rchip[2 * q + 1, dx, 32:64]
            for dy in range(1, 4):
                total = total + rb1[2 * q + 1 - dy % 2, dy // 2, dx].astype(F32)
            sb2[q, dx] = total
        for d in range(1, 4):
            a2_copy(q, d).start()
            b2_copy(q, d).start()

    def third_stage(q):
        for d in range(1, 4):
            a2_copy(q, d).wait_recv()
            b2_copy(q, d).wait_recv()
        low, high = sa2[q, 0], sb2[q, 0]
        for d in range(1, 4):
            low = low + ra2[q, d]
            high = high + rb2[q, d]
        zsend[q, 0] = low[0:16]
        zsend[q, 1] = low[16:32]
        zsend[q, 2] = high[0:16]
        zsend[q, 3] = high[16:32]
        zr, kk = 1 - q // 4, q % 4
        for dz in range(1, 4):
            z_copy(q, dz).start()

        @pl.when(zr == 1)
        def _():
            z_copy(q, 0).start()

        @pl.when(zr == 0)
        def _():
            rz[kk, 0] = zsend[q, zh]

    def steps(m, carry):
        n = 2 * m
        chip_sum(n - 2)
        contract(n, xz_tiles, False)
        chip_copy(n).start()
        first_stage(n - 2)

        @pl.when(n >= 6)
        def _():
            second_stage(m - 3)

        chip_sum(n - 1)
        contract(n + 1, xz_tiles, False)
        chip_copy(n + 1).start()
        first_stage(n - 1)

        @pl.when(n >= 8)
        def _():
            third_stage(m - 4)

        return carry

    def opening(n, carry):
        contract(n, xz_tiles, False)
        chip_copy(n).start()
        return carry

    lax.fori_loop(0, 2, opening, 0)
    lax.fori_loop(1, PASSES // 2, steps, 0)
    chip_sum(14)
    first_stage(14)

    second_stage(5)
    third_stage(4)
    chip_sum(15)
    first_stage(15)
    second_stage(6)
    third_stage(5)
    second_stage(7)
    third_stage(6)
    third_stage(7)

    for q in range(8):
        for dz in range(0 if q < 4 else 1, 4):
            z_copy(q, dz).wait_recv()
    for kk in range(4):
        total = rz[kk, 0]
        for s in range(1, 8):
            total = total + rz[kk, s]
        out[kk] = total * WEIGHT

    def drain(n, carry):
        chip_copy(n).wait_send()
        for dx in range(1, 4):
            a1_copy(n, dx).wait_send()
        b1_copy(n, 1).wait_send()

        @pl.when(n % 2 == 0)
        def _():
            b1_copy(n, 0).wait_send()

        return carry

    lax.fori_loop(0, PASSES, drain, 0)
    for q in range(8):
        for d in range(1, 4):
            a2_copy(q, d).wait_send()
            b2_copy(q, d).wait_send()
        for dz in range(0 if q < 4 else 1, 4):
            z_copy(q, dz).wait_send()


def per_device(modes, wall_grad):
    phi5 = jnp.transpose(modes, (0, 1, 3, 2, 4))
    wall5 = jnp.transpose(wall_grad, (0, 1, 3, 2, 4))
    vm = pl.BlockSpec(memory_space=pltpu.VMEM)
    dma = pltpu.SemaphoreType.DMA
    return pl.pallas_call(
        kernel,
        out_shape=jax.ShapeDtypeStruct((4, 16, M), F32),
        in_specs=[vm] * 2,
        out_specs=vm,
        scratch_shapes=[
            pltpu.VMEM((2, 3, 80, M), BF),
            pltpu.VMEM((2, 3, 3, 48, M), BF),
            pltpu.VMEM((2, 3, 3, 48, M), BF),
            pltpu.VMEM((3, 80, M), BF),
            pltpu.VMEM((3, 80, M), BF),
            pltpu.VMEM((72, 64, M), F32),
            pltpu.VMEM((2, 3, POINTS, M), BF),
            pltpu.VMEM((5, 3, M, 256), BF),
            pltpu.VMEM((14, 3, M, 256), F32),
            pltpu.VMEM((PASSES, 8, 2, 64, M), F32),
            pltpu.VMEM((PASSES, 8, 64, M), F32),
            pltpu.VMEM((PASSES, 4, 2, 32, M), BF),
            pltpu.VMEM((PASSES, 2, 4, 32, M), BF),
            pltpu.VMEM((PASSES, 4, 2, 32, M), BF),
            pltpu.VMEM((PASSES, 2, 4, 32, M), BF),
            pltpu.VMEM((8, 4, 32, M), F32),
            pltpu.VMEM((8, 4, 32, M), F32),
            pltpu.VMEM((8, 4, 32, M), F32),
            pltpu.VMEM((8, 4, 32, M), F32),
            pltpu.VMEM((8, 4, 16, M), F32),
            pltpu.VMEM((4, 8, 16, M), F32),
            dma((4,)), dma((4,)),
            dma((PASSES,)), dma((PASSES,)),
            dma((PASSES, 4)), dma((PASSES, 4)),
            dma((PASSES, 2)), dma((PASSES, 2)),
            dma((8, 4)), dma((8, 4)),
            dma((8, 4)), dma((8, 4)),
            dma((8, 4)), dma((8, 4)),
        ],
        compiler_params=pltpu.CompilerParams(
            collective_id=0, has_side_effects=True, vmem_limit_bytes=56 * 2**20),
        cost_estimate=pl.CostEstimate(
            flops=2 * 128 * 3456 * 16384, bytes_accessed=4 * 2**20, transcendentals=0),
    )(phi5, wall5)


def solution(mesh):
    placed = (P(None, "gx", "gz", None, None), P(None, "gx", "gz", None, None))
    body = jax.shard_map(
        per_device, mesh=mesh, in_specs=placed, out_specs=P("gx", "gz", None), check_vma=False)

    def run(modes, wall_grad):
        with jax.sharding.use_abstract_mesh(mesh.abstract_mesh):
            return body(modes, wall_grad)

    return run
```
